512 devices in a mesh: tm: 16 (over z), chan: 16 (over y_lo, x, core), freq: 2 (over y_hi).
Axes of the slice: x: 4, y: 4 (y_hi: 2, y_lo: 2; y = y_hi * 2 + y_lo), z: 16, core: 2. Of those that a mesh axis runs over, the one named last changes fastest.
Arguments:
- raw_record: bfloat16 [32, 4096, 4096], P(('tm', 'freq'), 'chan'), may hold values from -6 to 6
- good_mask: int32 [4096], P('chan'), may hold values 0 or 1
- reach_limit: int32 [4096], P('chan'), may hold values from 128 to 511
Outputs:
- stacked_cross: bfloat16 [2, 128, 4096, 512], P(None, ('tm', 'freq'), 'chan')
The draws below stay inside these ranges and needn't reach their ends.
All inputs are finite; a program needn't handle non-finite values. No bound on the sum of `good_mask` on one device may be relied on, other than what follows from the above.
Results may differ from the reference program's by a relative error of at most 0.0066.
Values may be sent and summed in bfloat16 or wider, within the bound.
A program may use at most 64 MiB of HBM per device.

```python
import jax
import jax.numpy as jnp
from jax import lax

CHD = 256
L = 4096
K = 512
F0 = 64
CH = 4096
NF = 128
WINDOWS = 32
N_CHAN = 16


def with_ends(entries, own_key, low, largest):
    place = [jax.random.randint(jax.random.fold_in(own_key, axis), (), 0, length) for axis, length in enumerate(entries.shape)]
    widest = entries.shape.index(max(entries.shape))
    neighbour = place[:widest] + [(place[widest] + 1) % entries.shape[widest]] + place[widest + 1:]
    return entries.at[tuple(place)].set(low).at[tuple(neighbour)].set(largest)


def steps_of(rng, dims, cuts, low, largest):
    def one(dim, blocks):
        steps = jax.random.uniform(jax.random.fold_in(jax.random.fold_in(rng, 6), dim), (blocks,), jnp.float32, low / len(cuts), largest / len(cuts))
        return jnp.repeat(jnp.exp(steps), dims[dim] // blocks).reshape((-1,) + (1,) * (len(dims) - dim - 1))

    factor_of = one(*cuts[0])
    for cut in cuts[1:]:
        factor_of = factor_of * one(*cut)
    return factor_of


def bell_draw(key, dims, deviation, most, shards=(), kind=jnp.bfloat16):
    values = deviation * jax.random.normal(key, dims, jnp.float32)
    if shards:
        values = values * steps_of(key, dims, shards, -0.22, 0.18)
    return jnp.clip(values, -most, most).astype(kind)


def setup_inputs(seed: int = 0) -> dict:
    splits = jax.random.split(jax.random.key(seed), 4)
    return {
        "raw_record": bell_draw(splits[0], (WINDOWS, CH, L), 1.0, 6.0, ((0, 32), (1, 16))),
        "good_mask": with_ends((jax.random.randint(splits[1], (CH,), 0, 8) < 7).astype(jnp.int32), jax.random.fold_in(splits[1], 1), 0, 1),
        "reach_limit": with_ends(jax.random.randint(splits[2], (CH,), K // 4, K), jax.random.fold_in(splits[2], 1), K // 4, K - 1).astype(jnp.int32),
    }


def build_table():
    bins = F0 + jnp.arange(NF, dtype=jnp.int32)
    times = jnp.arange(L, dtype=jnp.int32)
    phase = 2.0 * jnp.pi * (bins[:, None] * times[None, :] % L).astype(jnp.float32) / L
    taper = 0.5 - 0.5 * jnp.cos(2.0 * jnp.pi * times.astype(jnp.float32) / L)
    real_part = taper[None, :] * jnp.cos(phase)
    imag_part = -taper[None, :] * jnp.sin(phase)
    return jnp.concatenate([real_part, imag_part], axis=0).T.astype(jnp.bfloat16)

def reference(raw_record, good_mask, reach_limit):
    table = build_table().astype(jnp.float32)
    mask_float = good_mask.astype(jnp.float32)

    def whiten_one(window):
        spectrum = jnp.dot(window.astype(jnp.float32), table, precision=lax.Precision.HIGHEST)
        power = lax.optimization_barrier(jnp.sum(spectrum * spectrum, axis=1)) / NF
        scaled = spectrum * (lax.rsqrt(power + 1e-06) * mask_float)[:, None]
        return scaled.astype(jnp.bfloat16)
    whites = lax.map(whiten_one, raw_record)
    spectra = whites.reshape(WINDOWS, CH, 2, NF).transpose(3, 2, 0, 1)
    spectra = jnp.pad(spectra, ((0, 0), (0, 0), (0, 0), (0, K)))
    offsets = jnp.arange(K, dtype=jnp.int32)
    width = CHD + K

    def per_bin(pieces):
        left_full = jnp.concatenate([pieces[0], pieces[1]], axis=0).astype(jnp.float32)
        imag_full = jnp.concatenate([pieces[1], -pieces[0]], axis=0).astype(jnp.float32)

        def per_block(block):
            start = (block * CHD).astype(jnp.int32)
            zero = jnp.zeros((), jnp.int32)
            left = lax.dynamic_slice(left_full, (zero, start), (2 * WINDOWS, CHD))
            right_real = lax.dynamic_slice(left_full, (zero, start), (2 * WINDOWS, width))
            right_imag = lax.dynamic_slice(imag_full, (zero, start), (2 * WINDOWS, width))
            gram = jnp.stack([jnp.dot(left.T, right_real, precision=lax.Precision.HIGHEST), jnp.dot(left.T, right_imag, precision=lax.Precision.HIGHEST)])
            flat = jnp.pad(gram.reshape(2, CHD * width), ((0, 0), (0, CHD)))
            band = flat.reshape(2, CHD, width + 1)[:, :, :K]
            limits = lax.dynamic_slice(reach_limit, (start,), (CHD,))
            keep = offsets[None, :] <= limits[:, None]
            return jnp.where(keep[None], band, 0.0).astype(jnp.bfloat16)
        blocks = lax.map(per_block, jnp.arange(N_CHAN, dtype=jnp.int32))
        return blocks.transpose(1, 0, 2, 3).reshape(2, CH, K)
    result = lax.map(per_bin, spectra)
    return result.transpose(1, 0, 2, 3)
```

```python
import functools

import jax
import jax.numpy as jnp
import numpy as np
from jax import lax
from jax.experimental import pallas as pl
from jax.experimental.pallas import tpu as pltpu
from jax.sharding import PartitionSpec as P

K = 512
F0 = 64
FB_DEV = 4
ROWS = 2 * FB_DEV
LANES = 128
TIME_CHUNKS = 4
PARTS = 4
MESH = pl.DeviceIdType.MESH


def build_rows(groups, length):
    bins = F0 + np.arange(groups * FB_DEV, dtype=np.int64)
    times = np.arange(length, dtype=np.int64)
    turn = np.float32(2.0 * np.pi)
    phase = turn * ((bins[:, None] * times[None, :]) % length).astype(np.float32) / np.float32(length)
    taper = np.float32(0.5) - np.float32(0.5) * np.cos(turn * times.astype(np.float32) / np.float32(length))
    real_part = (taper[None, :] * np.cos(phase)).reshape(groups, FB_DEV, length)
    imag_part = (-taper[None, :] * np.sin(phase)).reshape(groups, FB_DEV, length)
    rows = np.stack([real_part, imag_part], axis=1).reshape(groups * ROWS, length)
    return rows.reshape(groups * ROWS, length // LANES, LANES).transpose(1, 0, 2).astype(jnp.bfloat16)


def ring_order(count):
    return sorted(range(1, count), key=lambda d: -min(d, count - d))


def exchange_kernel(tm_count, chan_count, freq_count, table_ref, raw_ref, mask_ref, out_ref,
                    table_v, raw_v, mask_v, send_v, recv_v, load_sem, mask_sem, send_sem, recv_sem, ahead_send, ahead_recv, out_sem):
    tm, chan, freq = lax.axis_index("tm"), lax.axis_index("chan"), lax.axis_index("freq")
    groups = tm_count * freq_count
    peers = [(dt, df) for dt in ring_order(tm_count) for df in range(freq_count)]
    peers += [(0, df) for df in range(1, freq_count)]

    def place(dt, df):
        return lax.rem(tm + dt, tm_count), lax.rem(freq + df, freq_count)

    barrier = pltpu.get_barrier_semaphore()
    for dt, df in peers:
        t, f = place(dt, df)
        pl.semaphore_signal(barrier, inc=1, device_id=(t, chan, f), device_id_type=MESH)
    for up in (1, 2):
        @pl.when(chan + up < chan_count)
        def _():
            pl.semaphore_signal(barrier, inc=1, device_id=(tm, chan + up, freq), device_id_type=MESH)

    length = raw_ref.shape[1]
    step = length // TIME_CHUNKS
    loads = []
    for i in range(TIME_CHUNKS):
        span = pl.ds(i * step, step)
        runs = pl.ds(i * step // LANES, step // LANES)
        loads.append((
            pltpu.make_async_copy(table_ref.at[runs], table_v.at[runs], load_sem.at[0, i]),
            pltpu.make_async_copy(raw_ref.at[:, span], raw_v.at[:, span], load_sem.at[1, i]),
        ))
    for pair in loads:
        for copy in pair:
            copy.start()
    mask_copy = pltpu.make_async_copy(mask_ref, mask_v, mask_sem)
    mask_copy.start()

    for up in (1, 2):
        @pl.when(chan + up >= chan_count)
        def _():
            recv_v[up] = jnp.zeros(recv_v.shape[1:], recv_v.dtype)

    spectrum = None
    for i, pair in enumerate(loads):
        for copy in pair:
            copy.wait()
        span = slice(i * step, (i + 1) * step)
        rows = jnp.concatenate([table_v[j] for j in range(i * step // LANES, (i + 1) * step // LANES)], axis=1)
        term = lax.dot_general(
            rows, raw_v[:, span], (((1,), (1,)), ((), ())), preferred_element_type=jnp.float32
        )
        spectrum = term if spectrum is None else spectrum + term
    power = jnp.sum(spectrum * spectrum, axis=0, keepdims=True) / (groups * FB_DEV)
    mask_copy.wait()
    factor = lax.rsqrt(power + 1e-06) * mask_v[...].astype(jnp.float32)
    white = (spectrum * factor).reshape(groups, ROWS, 2 * LANES)
    tiles = jnp.concatenate([white[:, :, :LANES], white[:, :, LANES:]], axis=1)
    send_v[...] = tiles.astype(jnp.bfloat16)

    def part_of(slot):
        return slot * PARTS // groups

    own = tm * freq_count + freq
    recv_v[0, 0] = send_v[own]

    pl.semaphore_wait(barrier, groups - 1 + jnp.minimum(chan, 2))
    sends = []
    for dt, df in peers:
        t, f = place(dt, df)
        slot = ((-dt) % tm_count) * freq_count + (-df) % freq_count
        copy = pltpu.make_async_remote_copy(
            src_ref=send_v.at[t * freq_count + f],
            dst_ref=recv_v.at[0, slot],
            send_sem=send_sem,
            recv_sem=recv_sem.at[part_of(slot)],
            device_id=(t, chan, f),
            device_id_type=MESH,
        )
        copy.start()
        sends.append(copy)

    per_part = groups // PARTS

    def ahead(up, q):
        span = pl.ds(q * per_part, per_part)
        return pltpu.make_async_remote_copy(
            src_ref=recv_v.at[0, span],
            dst_ref=recv_v.at[up, span],
            send_sem=ahead_send.at[up - 1, q],
            recv_sem=ahead_recv.at[up - 1, q],
            device_id=(tm, chan - up, freq),
            device_id_type=MESH,
        )

    def store(block, q):
        span = pl.ds(q * per_part, per_part)
        return pltpu.make_async_copy(recv_v.at[block, span], out_ref.at[block, span], out_sem.at[block, q])

    for q in range(PARTS):
        lo = 1 if q == 0 else q * per_part
        span = pl.ds(lo, (q + 1) * per_part - lo)
        pltpu.make_async_copy(recv_v.at[0, span], recv_v.at[0, span], recv_sem.at[q]).wait()
        for up in (1, 2):
            @pl.when(chan >= up)
            def _():
                ahead(up, q).start()
        store(0, q).start()
    for q in range(PARTS):
        for up in (1, 2):
            @pl.when(chan + up < chan_count)
            def _():
                ahead(up, q).wait_recv()
            store(up, q).start()
    rest = pl.ds(1, groups - 1)
    pltpu.make_async_copy(send_v.at[rest], send_v.at[rest], send_sem).wait()
    for q in range(PARTS):
        for up in (1, 2):
            @pl.when(chan >= up)
            def _():
                ahead(up, q).wait_send()
        for block in range(3):
            store(block, q).wait()


def exchange(table, raw, mask, tm_count, chan_count, freq_count):
    groups = tm_count * freq_count
    width, length = raw.shape
    return pl.pallas_call(
        functools.partial(exchange_kernel, tm_count, chan_count, freq_count),
        out_shape=jax.ShapeDtypeStruct((3, groups, 2 * ROWS, LANES), jnp.bfloat16),
        in_specs=[
            pl.BlockSpec(memory_space=pltpu.HBM),
            pl.BlockSpec(memory_space=pltpu.HBM),
            pl.BlockSpec(memory_space=pltpu.HBM),
        ],
        out_specs=pl.BlockSpec(memory_space=pl.ANY),
        scratch_shapes=[
            pltpu.VMEM(table.shape, jnp.bfloat16),
            pltpu.VMEM((width, length), jnp.bfloat16),
            pltpu.VMEM((1, width), jnp.int32),
            pltpu.VMEM((groups, 2 * ROWS, LANES), jnp.bfloat16),
            pltpu.VMEM((3, groups, 2 * ROWS, LANES), jnp.bfloat16),
            pltpu.SemaphoreType.DMA((2, TIME_CHUNKS)),
            pltpu.SemaphoreType.DMA,
            pltpu.SemaphoreType.DMA,
            pltpu.SemaphoreType.DMA((PARTS,)),
            pltpu.SemaphoreType.DMA((2, PARTS)),
            pltpu.SemaphoreType.DMA((2, PARTS)),
            pltpu.SemaphoreType.DMA((3, PARTS)),
        ],
        compiler_params=pltpu.CompilerParams(
            collective_id=0, has_side_effects=True, vmem_limit_bytes=60 << 20
        ),
        name="exchange",
    )(table, raw, mask)


def band_kernel(blocks_ref, reach_ref, out_ref, right_v, left_v, reach_v):
    depth = right_v.shape[0]
    groups = depth // ROWS
    index = pl.program_id(0)

    @pl.when(index == 0)
    def _():
        halves = []
        for block in range(3):
            tiles = blocks_ref[block].astype(jnp.float32)
            for half in range(2):
                halves.append(tiles[:, half * ROWS:(half + 1) * ROWS, :])
        for j, half in enumerate(halves):
            right_v[:, j * LANES:(j + 1) * LANES] = half.reshape(depth, LANES).astype(jnp.bfloat16)
        row = lax.broadcasted_iota(jnp.int32, (groups, ROWS, LANES), 1)
        for j in range(2):
            span = slice(j * LANES, (j + 1) * LANES)
            left_v[0, span, :] = halves[j].reshape(depth, LANES).T
            turned = jnp.concatenate([-halves[j][:, FB_DEV:], halves[j][:, :FB_DEV]], axis=1)
            left_v[1, span, :] = turned.reshape(depth, LANES).T
        reach_v[...] = jnp.broadcast_to(reach_ref[...], (LANES, 2 * LANES)).T

    part = index // FB_DEV
    which = lax.rem(index, FB_DEV)
    column = lax.broadcasted_iota(jnp.int32, (2 * LANES, depth), 1)
    left = jnp.where(lax.rem(column, FB_DEV) == which, left_v[part], 0.0).astype(jnp.bfloat16)
    row = lax.broadcasted_iota(jnp.int32, (LANES, LANES), 0)
    lane = lax.broadcasted_iota(jnp.int32, (LANES, LANES), 1)
    for half in range(2):
        rows = slice(half * LANES, (half + 1) * LANES)
        reach = reach_v[rows, :]
        count = K // LANES + 1
        turned = []
        for j in range(count):
            at = (half + j) * LANES
            product = jnp.dot(left[rows], right_v[:, at:at + LANES], preferred_element_type=jnp.float32)
            turned.append(jnp.take_along_axis(product, lax.rem(lane + row, LANES), axis=1, mode="promise_in_bounds"))
        for j in range(count - 1):
            band = jnp.where(lane + row < LANES, turned[j], turned[j + 1])
            band = jnp.where(lane + j * LANES <= reach, band, 0.0)
            out_ref[0, 0, rows, j * LANES:(j + 1) * LANES] = band.astype(out_ref.dtype)


def band_of(blocks, reach):
    groups = blocks.shape[1]
    depth = groups * ROWS
    return pl.pallas_call(
        band_kernel,
        grid=(2 * FB_DEV,),
        out_shape=jax.ShapeDtypeStruct((2, FB_DEV, 2 * LANES, K), jnp.bfloat16),
        in_specs=[
            pl.BlockSpec(blocks.shape, lambda i: (0, 0, 0, 0)),
            pl.BlockSpec((1, 2 * LANES), lambda i: (0, 0)),
        ],
        out_specs=pl.BlockSpec((1, 1, 2 * LANES, K), lambda i: (i // FB_DEV, i % FB_DEV, 0, 0)),
        scratch_shapes=[
            pltpu.VMEM((depth, 6 * LANES), jnp.bfloat16),
            pltpu.VMEM((2, 2 * LANES, depth), jnp.float32),
            pltpu.VMEM((2 * LANES, LANES), jnp.int32),
        ],
        name="band",
    )(blocks, reach)


def body(table, raw_record, good_mask, reach_limit):
    tm_count, chan_count, freq_count = (lax.axis_size(a) for a in ("tm", "chan", "freq"))
    width = raw_record.shape[1]
    blocks = exchange(table, raw_record[0], good_mask.reshape(1, width), tm_count, chan_count, freq_count)
    return band_of(blocks, reach_limit.reshape(1, width))


def solution(mesh):
    groups = mesh.shape["tm"] * mesh.shape["freq"]
    sharded = jax.shard_map(
        body,
        mesh=mesh,
        in_specs=(P(), P(("tm", "freq"), "chan", None), P("chan"), P("chan")),
        out_specs=P(None, ("tm", "freq"), "chan", None),
        check_vma=False,
    )

    def run(raw_record, good_mask, reach_limit):
        table = jnp.asarray(build_rows(groups, raw_record.shape[2]))
        return sharded(table, raw_record, good_mask, reach_limit)

    return run
```

```python
import functools

import jax
import jax.numpy as jnp
import numpy as np
from jax import lax
from jax.experimental import pallas as pl
from jax.experimental.pallas import tpu as pltpu
from jax.sharding import PartitionSpec as P

K = 512
F0 = 64
FB_DEV = 4
ROWS = 2 * FB_DEV
LANES = 128
TIME_CHUNKS = 4
PARTS = 4
MESH = pl.DeviceIdType.MESH


def build_rows(groups, length):
    bins = F0 + np.arange(groups * FB_DEV, dtype=np.int64)
    times = np.arange(length, dtype=np.int64)
    turn = np.float32(2.0 * np.pi)
    phase = turn * ((bins[:, None] * times[None, :]) % length).astype(np.float32) / np.float32(length)
    taper = np.float32(0.5) - np.float32(0.5) * np.cos(turn * times.astype(np.float32) / np.float32(length))
    real_part = (taper[None, :] * np.cos(phase)).reshape(groups, FB_DEV, length)
    imag_part = (-taper[None, :] * np.sin(phase)).reshape(groups, FB_DEV, length)
    rows = np.stack([real_part, imag_part], axis=1).reshape(groups * ROWS, length)
    return rows.reshape(groups * ROWS, length // LANES, LANES).transpose(1, 0, 2).astype(jnp.bfloat16)


def rank_of(distance, count):
    return jnp.maximum(jnp.minimum(2 * distance - 1, 2 * (count - distance)), 0)


def exchange_kernel(tm_count, chan_count, freq_count, table_ref, raw_ref, mask_ref, blocks_ref,
                    table_v, raw_v, mask_v, send_v, load_sem, mask_sem, send_sem, recv_sem, ahead_send, ahead_recv):
    tm, chan, freq = lax.axis_index("tm"), lax.axis_index("chan"), lax.axis_index("freq")
    groups = tm_count * freq_count
    per_part = groups // PARTS

    peers = [(tm, lax.rem(freq + df, freq_count), 0, df) for df in range(1, freq_count)]
    for k in range(tm_count - 1):
        t = k + jnp.minimum(jnp.maximum(k + 1 - tm, 0), 1)
        rank = rank_of(lax.rem(tm - t + tm_count, tm_count), tm_count)
        peers += [(t, lax.rem(freq + df, freq_count), rank, df) for df in range(freq_count)]

    length = raw_ref.shape[1]
    step = length // TIME_CHUNKS
    loads = []
    for i in range(TIME_CHUNKS):
        span = pl.ds(i * step, step)
        runs = pl.ds(i * step // LANES, step // LANES)
        loads.append((
            pltpu.make_async_copy(table_ref.at[runs], table_v.at[runs], load_sem.at[0, i]),
            pltpu.make_async_copy(raw_ref.at[:, span], raw_v.at[:, span], load_sem.at[1, i]),
        ))
    for pair in loads:
        for copy in pair:
            copy.start()
    mask_copy = pltpu.make_async_copy(mask_ref, mask_v, mask_sem)
    mask_copy.start()

    barrier = pltpu.get_barrier_semaphore()
    for t, f, _, _ in peers:
        pl.semaphore_signal(barrier, inc=1, device_id=(t, chan, f), device_id_type=MESH)
    for up in (1, 2):
        @pl.when(chan + up < chan_count)
        def _():
            pl.semaphore_signal(barrier, inc=1, device_id=(tm, chan + up, freq), device_id_type=MESH)

    for up in (1, 2):
        @pl.when(chan + up >= chan_count)
        def _():
            blocks_ref[up] = jnp.zeros(blocks_ref.shape[1:], blocks_ref.dtype)

    spectrum = None
    for i, pair in enumerate(loads):
        for copy in pair:
            copy.wait()
        rows = jnp.concatenate([table_v[j] for j in range(i * step // LANES, (i + 1) * step // LANES)], axis=1)
        term = lax.dot_general(
            rows, raw_v[:, i * step:(i + 1) * step], (((1,), (1,)), ((), ())), preferred_element_type=jnp.float32
        )
        spectrum = term if spectrum is None else spectrum + term
    power = jnp.sum(spectrum * spectrum, axis=0, keepdims=True) / (groups * FB_DEV)
    mask_copy.wait()
    factor = lax.rsqrt(power + 1e-06) * mask_v[...].astype(jnp.float32)
    white = (spectrum * factor).reshape(groups, ROWS, 2 * LANES)
    tiles = jnp.concatenate([white[:, :, :LANES], white[:, :, LANES:]], axis=1)
    send_v[...] = tiles.astype(jnp.bfloat16)

    pl.semaphore_wait(barrier, groups - 1 + jnp.minimum(chan, 2))
    for t, f, rank, df in peers:
        pltpu.make_async_remote_copy(
            src_ref=send_v.at[t * freq_count + f],
            dst_ref=blocks_ref.at[0, rank * freq_count + df],
            send_sem=send_sem,
            recv_sem=recv_sem.at[rank * freq_count // per_part],
            device_id=(t, chan, f),
            device_id_type=MESH,
        ).start()
    blocks_ref[0, 0] = send_v[tm * freq_count + freq]

    def ahead(up, q):
        span = pl.ds(q * per_part, per_part)
        return pltpu.make_async_remote_copy(
            src_ref=blocks_ref.at[0, span],
            dst_ref=blocks_ref.at[up, span],
            send_sem=ahead_send.at[up - 1, q],
            recv_sem=ahead_recv.at[up - 1, q],
            device_id=(tm, chan - up, freq),
            device_id_type=MESH,
        )

    for q in range(PARTS):
        lo = 1 if q == 0 else q * per_part
        span = pl.ds(lo, (q + 1) * per_part - lo)
        pltpu.make_async_copy(blocks_ref.at[0, span], blocks_ref.at[0, span], recv_sem.at[q]).wait()
        for up in (2, 1):
            @pl.when(chan >= up)
            def _():
                ahead(up, q).start()
    for q in range(PARTS):
        for up in (1, 2):
            @pl.when(chan + up < chan_count)
            def _():
                ahead(up, q).wait_recv()
    rest = pl.ds(1, groups - 1)
    pltpu.make_async_copy(send_v.at[rest], send_v.at[rest], send_sem).wait()
    for q in range(PARTS):
        for up in (1, 2):
            @pl.when(chan >= up)
            def _():
                ahead(up, q).wait_send()


def exchange(table, raw, mask, tm_count, chan_count, freq_count):
    groups = tm_count * freq_count
    width, length = raw.shape
    return pl.pallas_call(
        functools.partial(exchange_kernel, tm_count, chan_count, freq_count),
        out_shape=pltpu.VMEM((3, groups, 2 * ROWS, LANES), jnp.bfloat16),
        in_specs=[pl.BlockSpec(memory_space=pltpu.HBM)] * 3,
        out_specs=pl.BlockSpec(memory_space=pltpu.VMEM),
        scratch_shapes=[
            pltpu.VMEM(table.shape, jnp.bfloat16),
            pltpu.VMEM((width, length), jnp.bfloat16),
            pltpu.VMEM((1, width), jnp.int32),
            pltpu.VMEM((groups, 2 * ROWS, LANES), jnp.bfloat16),
            pltpu.SemaphoreType.DMA((2, TIME_CHUNKS)),
            pltpu.SemaphoreType.DMA,
            pltpu.SemaphoreType.DMA,
            pltpu.SemaphoreType.DMA((PARTS,)),
            pltpu.SemaphoreType.DMA((2, PARTS)),
            pltpu.SemaphoreType.DMA((2, PARTS)),
        ],
        compiler_params=pltpu.CompilerParams(
            collective_id=0, has_side_effects=True, vmem_limit_bytes=16 << 20
        ),
        name="exchange",
    )(*(pltpu.with_memory_space_constraint(x, pltpu.HBM) for x in (table, raw, mask)))


def channel_of(row):
    return row // 8 * 8 + 7 - row % 8


def band_kernel(blocks_ref, reach_ref, out_ref, right_v, left_v, reach_v, band_v, out_sem):
    depth = right_v.shape[0]
    row = lax.broadcasted_iota(jnp.int32, (LANES, LANES), 0)
    lane = lax.broadcasted_iota(jnp.int32, (LANES, LANES), 1)
    order = (channel_of(row) == lane).astype(jnp.bfloat16)
    for block in range(3):
        tiles = blocks_ref[block].astype(jnp.float32)
        for half in range(2):
            at = (2 * block + half) * LANES
            piece = tiles[:, half * ROWS:(half + 1) * ROWS, :]
            right_v[:, at:at + LANES] = piece.reshape(depth, LANES).astype(jnp.bfloat16)
            if block == 0:
                turned = jnp.concatenate([-piece[:, FB_DEV:], piece[:, :FB_DEV]], axis=1)
                for part, value in enumerate((piece, turned)):
                    left_v[part, at:at + LANES, :] = lax.dot_general(
                        order, value.reshape(depth, LANES).astype(jnp.bfloat16), (((1,), (1,)), ((), ())),
                        preferred_element_type=jnp.float32,
                    ).astype(jnp.bfloat16)
    reach_v[...] = jnp.broadcast_to(reach_ref[...], (LANES, 2 * LANES)).T

    column = lax.broadcasted_iota(jnp.int32, (LANES, depth), 1)
    backwards = 7 - lax.broadcasted_iota(jnp.int32, (8, LANES), 0)
    tiles = K // LANES
    copies = []
    for part in range(2):
        for which in range(FB_DEV):
            for half in range(2):
                rows = slice(half * LANES, (half + 1) * LANES)
                left = jnp.where(column % FB_DEV == which, left_v[part, rows, :], jnp.zeros((), jnp.bfloat16))
                product = jnp.concatenate([
                    jnp.dot(left, right_v[:, at:at + 2 * LANES], preferred_element_type=jnp.float32)
                    for at in range(0, 6 * LANES, 2 * LANES)
                ], axis=1)[:, half * LANES:half * LANES + K + LANES]
                for j in range(tiles):
                    here = product[:, j * LANES:(j + 1) * LANES]
                    beyond = product[:, (j + 1) * LANES:(j + 2) * LANES]
                    joined = jnp.where(lane >= channel_of(row), here, beyond)
                    band = jnp.concatenate([
                        jnp.take_along_axis(
                            pltpu.roll(joined[at:at + 8], (LANES - 7 - at) % LANES, 1, stride=1, stride_axis=0),
                            backwards, axis=0, mode="promise_in_bounds",
                        )
                        for at in range(0, LANES, 8)
                    ], axis=0)
                    band = jnp.where(lane + j * LANES <= reach_v[rows, :], band, 0.0)
                    band_v[part, which, rows, j * LANES:(j + 1) * LANES] = band.astype(jnp.bfloat16)
            copy = pltpu.make_async_copy(band_v.at[part, which], out_ref.at[part, which], out_sem.at[part, which])
            copy.start()
            copies.append(copy)
    for copy in copies:
        copy.wait()


def band_of(blocks, reach):
    depth = blocks.shape[1] * ROWS
    shape = (2, FB_DEV, 2 * LANES, K)
    return pl.pallas_call(
        band_kernel,
        out_shape=jax.ShapeDtypeStruct(shape, jnp.bfloat16),
        in_specs=[pl.BlockSpec(memory_space=pltpu.VMEM)] * 2,
        out_specs=pl.BlockSpec(memory_space=pl.ANY),
        scratch_shapes=[
            pltpu.VMEM((depth, 6 * LANES), jnp.bfloat16),
            pltpu.VMEM((2, 2 * LANES, depth), jnp.bfloat16),
            pltpu.VMEM((2 * LANES, LANES), jnp.int32),
            pltpu.VMEM(shape, jnp.bfloat16),
            pltpu.SemaphoreType.DMA((2, FB_DEV)),
        ],
        compiler_params=pltpu.CompilerParams(vmem_limit_bytes=32 << 20),
        name="band",
    )(blocks, reach)


def body(table, raw_record, good_mask, reach_limit):
    tm_count, chan_count, freq_count = (lax.axis_size(a) for a in ("tm", "chan", "freq"))
    width = raw_record.shape[1]
    blocks = exchange(table, raw_record[0], good_mask.reshape(1, width), tm_count, chan_count, freq_count)
    return band_of(blocks, reach_limit.reshape(1, width))


def solution(mesh):
    groups = mesh.shape["tm"] * mesh.shape["freq"]
    sharded = jax.shard_map(
        body,
        mesh=mesh,
        in_specs=(P(), P(("tm", "freq"), "chan", None), P("chan"), P("chan")),
        out_specs=P(None, ("tm", "freq"), "chan", None),
        check_vma=False,
    )

    def run(raw_record, good_mask, reach_limit):
        table = jnp.asarray(build_rows(groups, raw_record.shape[2]))
        return sharded(table, raw_record, good_mask, reach_limit)

    return run
```

```python
import functools

import jax
import jax.numpy as jnp
import numpy as np
from jax import lax
from jax.experimental import pallas as pl
from jax.experimental.pallas import tpu as pltpu
from jax.sharding import PartitionSpec as P

K = 512
F0 = 64
FB_DEV = 4
ROWS = 2 * FB_DEV
LANES = 128
TIME_CHUNKS = 4
PARTS = 4
MESH = pl.DeviceIdType.MESH


def build_rows(groups, length):
    bins = F0 + np.arange(groups * FB_DEV, dtype=np.int64)
    times = np.arange(length, dtype=np.int64)
    turn = np.float32(2.0 * np.pi)
    phase = turn * ((bins[:, None] * times[None, :]) % length).astype(np.float32) / np.float32(length)
    taper = np.float32(0.5) - np.float32(0.5) * np.cos(turn * times.astype(np.float32) / np.float32(length))
    real_part = (taper[None, :] * np.cos(phase)).reshape(groups, FB_DEV, length)
    imag_part = (-taper[None, :] * np.sin(phase)).reshape(groups, FB_DEV, length)
    rows = np.stack([real_part, imag_part], axis=1).reshape(groups * ROWS, length)
    return rows.reshape(groups * ROWS, length // LANES, LANES).transpose(1, 0, 2).astype(jnp.bfloat16)


def rank_of(distance, count):
    return jnp.maximum(jnp.minimum(2 * distance - 1, 2 * (count - distance)), 0)


def exchange_kernel(tm_count, chan_count, freq_count, table_ref, raw_ref, mask_ref, blocks_ref,
                    table_v, raw_v, mask_v, send_v, load_sem, mask_sem, send_sem, recv_sem, ahead_send, ahead_recv, relay_send, go_sem):
    tm, chan, freq = lax.axis_index("tm"), lax.axis_index("chan"), lax.axis_index("freq")
    groups = tm_count * freq_count
    per_part = groups // PARTS

    beside = [(tm, lax.rem(freq + df, freq_count), 0, df) for df in range(1, freq_count)]
    peers = []
    for k in range(tm_count - 1):
        t = k + jnp.minimum(jnp.maximum(k + 1 - tm, 0), 1)
        rank = rank_of(lax.rem(tm - t + tm_count, tm_count), tm_count)
        peers += [(t, lax.rem(freq + df, freq_count), rank, df) for df in range(freq_count)]

    low, high = 5 * tm_count // 16, 10 * tm_count // 16
    split = (low + high) // 2
    far = (tm >= low) & (tm < high)

    length = raw_ref.shape[1]
    step = length // TIME_CHUNKS
    loads = []
    for i in range(TIME_CHUNKS):
        span = pl.ds(i * step, step)
        runs = pl.ds(i * step // LANES, step // LANES)
        loads.append((
            pltpu.make_async_copy(table_ref.at[runs], table_v.at[runs], load_sem.at[0, i]),
            pltpu.make_async_copy(raw_ref.at[:, span], raw_v.at[:, span], load_sem.at[1, i]),
        ))
    for pair in loads:
        for copy in pair:
            copy.start()
    mask_copy = pltpu.make_async_copy(mask_ref, mask_v, mask_sem)
    mask_copy.start()

    barrier = pltpu.get_barrier_semaphore()

    def greet(t, f):
        pl.semaphore_signal(barrier, inc=1, device_id=(t, chan, f), device_id_type=MESH)

    @pl.when(tm < low)
    def _():
        for t, f, _, _ in beside + peers:
            greet(t, f)

    @pl.when(far)
    def _():
        for t in (*range(low), *range(high, tm_count)):
            for f in range(freq_count):
                greet(t, f)

    @pl.when(tm >= high)
    def _():
        for t in (*range(low), *range(high, tm_count - 1)):
            past = jnp.minimum(jnp.maximum(t + 1 - tm, 0), 1)
            for f in range(freq_count):
                greet(t + past, f)
        for t, f, _, _ in beside:
            greet(t, f)

    for up in (1, 2):
        @pl.when(chan + up < chan_count)
        def _():
            pl.semaphore_signal(barrier, inc=1, device_id=(tm, chan + up, freq), device_id_type=MESH)

    for up in (1, 2):
        @pl.when(chan + up >= chan_count)
        def _():
            blocks_ref[up] = jnp.zeros(blocks_ref.shape[1:], blocks_ref.dtype)

    spectrum = None
    for i, pair in enumerate(loads):
        for copy in pair:
            copy.wait()
        rows = jnp.concatenate([table_v[j] for j in range(i * step // LANES, (i + 1) * step // LANES)], axis=1)
        term = lax.dot_general(
            rows, raw_v[:, i * step:(i + 1) * step], (((1,), (1,)), ((), ())), preferred_element_type=jnp.float32
        )
        spectrum = term if spectrum is None else spectrum + term
    power = jnp.sum(spectrum * spectrum, axis=0, keepdims=True) / (groups * FB_DEV)
    mask_copy.wait()
    factor = lax.rsqrt(power + 1e-06) * mask_v[...].astype(jnp.float32)
    white = (spectrum * factor).reshape(groups, ROWS, 2 * LANES)
    tiles = jnp.concatenate([white[:, :, :LANES], white[:, :, LANES:]], axis=1)
    send_v[...] = tiles.astype(jnp.bfloat16)

    def send(some):
        for t, f, rank, df in some:
            pltpu.make_async_remote_copy(
                src_ref=send_v.at[t * freq_count + f],
                dst_ref=blocks_ref.at[0, rank * freq_count + df],
                send_sem=send_sem,
                recv_sem=recv_sem.at[rank * freq_count // per_part],
                device_id=(t, chan, f),
                device_id_type=MESH,
            ).start()

    def let_go(planes):
        for t in planes:
            pl.semaphore_signal(go_sem, inc=1, device_id=(t, chan, freq), device_id_type=MESH)

    @pl.when(far)
    def _():
        pl.semaphore_wait(barrier, low * freq_count + jnp.minimum(chan, 2))

    @pl.when(jnp.logical_not(far))
    def _():
        pl.semaphore_wait(barrier, groups - 1 + jnp.minimum(chan, 2))

    @pl.when(tm == low - 1)
    def _():
        let_go(range(low, split))

    @pl.when(tm == high)
    def _():
        let_go(range(split, high))

    send(peers[:low * freq_count])

    @pl.when(far)
    def _():
        pl.semaphore_wait(go_sem, 1)

    send(beside + peers[low * freq_count:])
    blocks_ref[0, 0] = send_v[tm * freq_count + freq]

    odd = lax.rem(chan, 2) == 1

    def ahead(up, q):
        span = pl.ds(q * per_part, per_part)
        return pltpu.make_async_remote_copy(
            src_ref=blocks_ref.at[0, span],
            dst_ref=blocks_ref.at[up, span],
            send_sem=ahead_send.at[up - 1, q],
            recv_sem=ahead_recv.at[up - 1, q],
            device_id=(tm, chan - up, freq),
            device_id_type=MESH,
        )

    for q in range(PARTS):
        lo = 1 if q == 0 else q * per_part
        span = pl.ds(lo, (q + 1) * per_part - lo)
        pltpu.make_async_copy(blocks_ref.at[0, span], blocks_ref.at[0, span], recv_sem.at[q]).wait()
        @pl.when(odd & (chan >= 2))
        def _():
            ahead(2, q).start()

        @pl.when(chan >= 1)
        def _():
            ahead(1, q).start()

    passing = odd & (chan + 1 < chan_count)

    def relay(q):
        span = pl.ds(q * per_part, per_part)
        return pltpu.make_async_remote_copy(
            src_ref=blocks_ref.at[1, span],
            dst_ref=blocks_ref.at[2, span],
            send_sem=relay_send.at[q],
            recv_sem=ahead_recv.at[1, q],
            device_id=(tm, chan - 1, freq),
            device_id_type=MESH,
        )

    @pl.when(passing)
    def _():
        for q in range(PARTS):
            ahead(1, q).wait_recv()
            relay(q).start()

    @pl.when(jnp.logical_not(odd))
    def _():
        for q in range(PARTS):
            ahead(1, q).wait_recv()

    @pl.when(chan + 2 < chan_count)
    def _():
        for q in range(PARTS):
            ahead(2, q).wait_recv()

    rest = pl.ds(1, groups - 1)
    pltpu.make_async_copy(send_v.at[rest], send_v.at[rest], send_sem).wait()

    @pl.when(chan >= 1)
    def _():
        for q in range(PARTS):
            ahead(1, q).wait_send()

    @pl.when(odd & (chan >= 2))
    def _():
        for q in range(PARTS):
            ahead(2, q).wait_send()

    @pl.when(passing)
    def _():
        for q in range(PARTS):
            relay(q).wait_send()


def exchange(table, raw, mask, tm_count, chan_count, freq_count):
    groups = tm_count * freq_count
    width, length = raw.shape
    return pl.pallas_call(
        functools.partial(exchange_kernel, tm_count, chan_count, freq_count),
        out_shape=pltpu.VMEM((3, groups, 2 * ROWS, LANES), jnp.bfloat16),
        in_specs=[pl.BlockSpec(memory_space=pltpu.HBM)] * 3,
        out_specs=pl.BlockSpec(memory_space=pltpu.VMEM),
        scratch_shapes=[
            pltpu.VMEM(table.shape, jnp.bfloat16),
            pltpu.VMEM((width, length), jnp.bfloat16),
            pltpu.VMEM((1, width), jnp.int32),
            pltpu.VMEM((groups, 2 * ROWS, LANES), jnp.bfloat16),
            pltpu.SemaphoreType.DMA((2, TIME_CHUNKS)),
            pltpu.SemaphoreType.DMA,
            pltpu.SemaphoreType.DMA,
            pltpu.SemaphoreType.DMA((PARTS,)),
            pltpu.SemaphoreType.DMA((2, PARTS)),
            pltpu.SemaphoreType.DMA((2, PARTS)),
            pltpu.SemaphoreType.DMA((PARTS,)),
            pltpu.SemaphoreType.REGULAR,
        ],
        compiler_params=pltpu.CompilerParams(
            collective_id=0, has_side_effects=True, vmem_limit_bytes=16 << 20
        ),
        name="exchange",
    )(*(pltpu.with_memory_space_constraint(x, pltpu.HBM) for x in (table, raw, mask)))


def channel_of(row):
    return row // 8 * 8 + 7 - row % 8


def band_kernel(blocks_ref, reach_ref, out_ref, right_v, left_v, reach_v, band_v, out_sem):
    depth = right_v.shape[0]
    row = lax.broadcasted_iota(jnp.int32, (LANES, LANES), 0)
    lane = lax.broadcasted_iota(jnp.int32, (LANES, LANES), 1)
    order = (channel_of(row) == lane).astype(jnp.bfloat16)
    for block in range(3):
        tiles = blocks_ref[block].astype(jnp.float32)
        for half in range(2):
            at = (2 * block + half) * LANES
            piece = tiles[:, half * ROWS:(half + 1) * ROWS, :]
            right_v[:, at:at + LANES] = piece.reshape(depth, LANES).astype(jnp.bfloat16)
            if block == 0:
                turned = jnp.concatenate([-piece[:, FB_DEV:], piece[:, :FB_DEV]], axis=1)
                for part, value in enumerate((piece, turned)):
                    left_v[part, at:at + LANES, :] = lax.dot_general(
                        order, value.reshape(depth, LANES).astype(jnp.bfloat16), (((1,), (1,)), ((), ())),
                        preferred_element_type=jnp.float32,
                    ).astype(jnp.bfloat16)
    reach_v[...] = jnp.broadcast_to(reach_ref[...], (LANES, 2 * LANES)).T

    column = lax.broadcasted_iota(jnp.int32, (LANES, depth), 1)
    backwards = 7 - lax.broadcasted_iota(jnp.int32, (8, LANES), 0)
    tiles = K // LANES
    copies = []
    for part in range(2):
        for which in range(FB_DEV):
            for half in range(2):
                rows = slice(half * LANES, (half + 1) * LANES)
                left = jnp.where(column % FB_DEV == which, left_v[part, rows, :], jnp.zeros((), jnp.bfloat16))
                product = jnp.concatenate([
                    jnp.dot(left, right_v[:, at:at + 2 * LANES], preferred_element_type=jnp.float32)
                    for at in range(0, 6 * LANES, 2 * LANES)
                ], axis=1)[:, half * LANES:half * LANES + K + LANES]
                for j in range(tiles):
                    here = product[:, j * LANES:(j + 1) * LANES]
                    beyond = product[:, (j + 1) * LANES:(j + 2) * LANES]
                    joined = jnp.where(lane >= channel_of(row), here, beyond)
                    band = jnp.concatenate([
                        jnp.take_along_axis(
                            pltpu.roll(joined[at:at + 8], (LANES - 7 - at) % LANES, 1, stride=1, stride_axis=0),
                            backwards, axis=0, mode="promise_in_bounds",
                        )
                        for at in range(0, LANES, 8)
                    ], axis=0)
                    band = jnp.where(lane + j * LANES <= reach_v[rows, :], band, 0.0)
                    band_v[part, which, rows, j * LANES:(j + 1) * LANES] = band.astype(jnp.bfloat16)
            copy = pltpu.make_async_copy(band_v.at[part, which], out_ref.at[part, which], out_sem.at[part, which])
            copy.start()
            copies.append(copy)
    for copy in copies:
        copy.wait()


def band_of(blocks, reach):
    depth = blocks.shape[1] * ROWS
    shape = (2, FB_DEV, 2 * LANES, K)
    return pl.pallas_call(
        band_kernel,
        out_shape=jax.ShapeDtypeStruct(shape, jnp.bfloat16),
        in_specs=[pl.BlockSpec(memory_space=pltpu.VMEM)] * 2,
        out_specs=pl.BlockSpec(memory_space=pl.ANY),
        scratch_shapes=[
            pltpu.VMEM((depth, 6 * LANES), jnp.bfloat16),
            pltpu.VMEM((2, 2 * LANES, depth), jnp.bfloat16),
            pltpu.VMEM((2 * LANES, LANES), jnp.int32),
            pltpu.VMEM(shape, jnp.bfloat16),
            pltpu.SemaphoreType.DMA((2, FB_DEV)),
        ],
        compiler_params=pltpu.CompilerParams(vmem_limit_bytes=32 << 20),
        name="band",
    )(blocks, reach)


def body(table, raw_record, good_mask, reach_limit):
    tm_count, chan_count, freq_count = (lax.axis_size(a) for a in ("tm", "chan", "freq"))
    width = raw_record.shape[1]
    blocks = exchange(table, raw_record[0], good_mask.reshape(1, width), tm_count, chan_count, freq_count)
    return band_of(blocks, reach_limit.reshape(1, width))


def solution(mesh):
    groups = mesh.shape["tm"] * mesh.shape["freq"]
    sharded = jax.shard_map(
        body,
        mesh=mesh,
        in_specs=(P(), P(("tm", "freq"), "chan", None), P("chan"), P("chan")),
        out_specs=P(None, ("tm", "freq"), "chan", None),
        check_vma=False,
    )

    def run(raw_record, good_mask, reach_limit):
        table = jnp.asarray(build_rows(groups, raw_record.shape[2]))
        return sharded(table, raw_record, good_mask, reach_limit)

    return run
```

```python
import functools

import jax
import jax.numpy as jnp
import numpy as np
from jax import lax
from jax.experimental import pallas as pl
from jax.experimental.pallas import tpu as pltpu
from jax.sharding import PartitionSpec as P

K = 512
F0 = 64
FB_DEV = 4
ROWS = 2 * FB_DEV
LANES = 128
TIME_CHUNKS = 4
PARTS = 4
MESH = pl.DeviceIdType.MESH


def build_rows(groups, length):
    bins = F0 + np.arange(groups * FB_DEV, dtype=np.int64)
    times = np.arange(length, dtype=np.int64)
    turn = np.float32(2.0 * np.pi)
    phase = turn * ((bins[:, None] * times[None, :]) % length).astype(np.float32) / np.float32(length)
    taper = np.float32(0.5) - np.float32(0.5) * np.cos(turn * times.astype(np.float32) / np.float32(length))
    real_part = (taper[None, :] * np.cos(phase)).reshape(groups, FB_DEV, length)
    imag_part = (-taper[None, :] * np.sin(phase)).reshape(groups, FB_DEV, length)
    rows = np.stack([real_part, imag_part], axis=1).reshape(groups * ROWS, length)
    return rows.reshape(groups * ROWS, length // LANES, LANES).transpose(1, 0, 2).astype(jnp.bfloat16)


def rank_of(distance, count):
    return jnp.maximum(jnp.minimum(2 * distance - 1, 2 * (count - distance)), 0)


def exchange_kernel(tm_count, chan_count, freq_count, table_ref, raw_ref, mask_ref, blocks_ref,
                    table_v, raw_v, mask_v, send_v, load_sem, mask_sem, send_sem, recv_sem, ahead_send, ahead_recv, relay_send, go_sem):
    tm, chan, freq = lax.axis_index("tm"), lax.axis_index("chan"), lax.axis_index("freq")
    groups = tm_count * freq_count
    per_part = groups // PARTS

    beside = [(tm, lax.rem(freq + df, freq_count), 0, df) for df in range(1, freq_count)]
    peers = []
    for k in range(tm_count - 1):
        t = k + jnp.minimum(jnp.maximum(k + 1 - tm, 0), 1)
        rank = rank_of(lax.rem(tm - t + tm_count, tm_count), tm_count)
        peers += [(t, lax.rem(freq + df, freq_count), rank, df) for df in range(freq_count)]

    low, high = 5 * tm_count // 16, 10 * tm_count // 16
    split = (low + high) // 2
    far = (tm >= low) & (tm < high)

    length = raw_ref.shape[1]
    step = length // TIME_CHUNKS
    loads = []
    for i in range(TIME_CHUNKS):
        span = pl.ds(i * step, step)
        runs = pl.ds(i * step // LANES, step // LANES)
        loads.append((
            pltpu.make_async_copy(table_ref.at[runs], table_v.at[runs], load_sem.at[0, i]),
            pltpu.make_async_copy(raw_ref.at[:, span], raw_v.at[:, span], load_sem.at[1, i]),
        ))
    for pair in loads:
        for copy in pair:
            copy.start()
    mask_copy = pltpu.make_async_copy(mask_ref, mask_v, mask_sem)
    mask_copy.start()

    barrier = pltpu.get_barrier_semaphore()

    def greet(t, f):
        pl.semaphore_signal(barrier, inc=1, device_id=(t, chan, f), device_id_type=MESH)

    @pl.when(tm < low)
    def _():
        for t, f, _, _ in beside + peers:
            greet(t, f)

    @pl.when(far)
    def _():
        for t in (*range(low), *range(high, tm_count)):
            for f in range(freq_count):
                greet(t, f)

    @pl.when(tm >= high)
    def _():
        for t in (*range(low), *range(high, tm_count - 1)):
            past = jnp.minimum(jnp.maximum(t + 1 - tm, 0), 1)
            for f in range(freq_count):
                greet(t + past, f)
        for t, f, _, _ in beside:
            greet(t, f)

    for up in (1, 2):
        @pl.when(chan + up < chan_count)
        def _():
            pl.semaphore_signal(barrier, inc=1, device_id=(tm, chan + up, freq), device_id_type=MESH)

    for up in (1, 2):
        @pl.when(chan + up >= chan_count)
        def _():
            blocks_ref[up] = jnp.zeros(blocks_ref.shape[1:], blocks_ref.dtype)

    spectrum = None
    for i, pair in enumerate(loads):
        for copy in pair:
            copy.wait()
        rows = jnp.concatenate([table_v[j] for j in range(i * step // LANES, (i + 1) * step // LANES)], axis=1)
        term = lax.dot_general(
            rows, raw_v[:, i * step:(i + 1) * step], (((1,), (1,)), ((), ())), preferred_element_type=jnp.float32
        )
        spectrum = term if spectrum is None else spectrum + term
    power = jnp.sum(spectrum * spectrum, axis=0, keepdims=True) / (groups * FB_DEV)
    mask_copy.wait()
    factor = lax.rsqrt(power + 1e-06) * mask_v[...].astype(jnp.float32)
    white = (spectrum * factor).reshape(groups, ROWS, 2 * LANES)
    tiles = jnp.concatenate([white[:, :, :LANES], white[:, :, LANES:]], axis=1)
    send_v[...] = tiles.astype(jnp.bfloat16)

    def send(some):
        for t, f, rank, df in some:
            pltpu.make_async_remote_copy(
                src_ref=send_v.at[t * freq_count + f],
                dst_ref=blocks_ref.at[0, rank * freq_count + df],
                send_sem=send_sem,
                recv_sem=recv_sem.at[rank * freq_count // per_part],
                device_id=(t, chan, f),
                device_id_type=MESH,
            ).start()

    def let_go(planes):
        for t in planes:
            pl.semaphore_signal(go_sem, inc=1, device_id=(t, chan, freq), device_id_type=MESH)

    @pl.when(far)
    def _():
        pl.semaphore_wait(barrier, low * freq_count + jnp.minimum(chan, 2))

    @pl.when(jnp.logical_not(far))
    def _():
        pl.semaphore_wait(barrier, groups - 1 + jnp.minimum(chan, 2))

    @pl.when(tm == low - 1)
    def _():
        let_go(range(low, split))

    @pl.when(tm == high)
    def _():
        let_go(range(split, high))

    send(peers[:low * freq_count])

    @pl.when(far)
    def _():
        pl.semaphore_wait(go_sem, 1)

    send(beside + peers[low * freq_count:])
    blocks_ref[0, 0] = send_v[tm * freq_count + freq]

    odd = lax.rem(chan, 2) == 1

    def ahead(up, q):
        span = pl.ds(q * per_part, per_part)
        return pltpu.make_async_remote_copy(
            src_ref=blocks_ref.at[0, span],
            dst_ref=blocks_ref.at[up, span],
            send_sem=ahead_send.at[up - 1, q],
            recv_sem=ahead_recv.at[up - 1, q],
            device_id=(tm, chan - up, freq),
            device_id_type=MESH,
        )

    for q in range(PARTS):
        lo = 1 if q == 0 else q * per_part
        span = pl.ds(lo, (q + 1) * per_part - lo)
        pltpu.make_async_copy(blocks_ref.at[0, span], blocks_ref.at[0, span], recv_sem.at[q]).wait()
        @pl.when(chan >= 1)
        def _():
            ahead(1, q).start()

        @pl.when((odd if q < PARTS - 1 else True) & (chan >= 2))
        def _():
            ahead(2, q).start()

    passing = odd & (chan + 1 < chan_count)

    def relay(q):
        span = pl.ds(q * per_part, per_part)
        return pltpu.make_async_remote_copy(
            src_ref=blocks_ref.at[1, span],
            dst_ref=blocks_ref.at[2, span],
            send_sem=relay_send.at[q],
            recv_sem=ahead_recv.at[1, q],
            device_id=(tm, chan - 1, freq),
            device_id_type=MESH,
        )

    @pl.when(passing)
    def _():
        for q in range(PARTS):
            ahead(1, q).wait_recv()
            if q < PARTS - 1:
                relay(q).start()

    @pl.when(jnp.logical_not(odd))
    def _():
        for q in range(PARTS):
            ahead(1, q).wait_recv()

    @pl.when(chan + 2 < chan_count)
    def _():
        for q in range(PARTS):
            ahead(2, q).wait_recv()

    rest = pl.ds(1, groups - 1)
    pltpu.make_async_copy(send_v.at[rest], send_v.at[rest], send_sem).wait()

    @pl.when(chan >= 1)
    def _():
        for q in range(PARTS):
            ahead(1, q).wait_send()

    @pl.when(odd & (chan >= 2))
    def _():
        for q in range(PARTS - 1):
            ahead(2, q).wait_send()

    @pl.when(chan >= 2)
    def _():
        ahead(2, PARTS - 1).wait_send()

    @pl.when(passing)
    def _():
        for q in range(PARTS - 1):
            relay(q).wait_send()


def exchange(table, raw, mask, tm_count, chan_count, freq_count):
    groups = tm_count * freq_count
    width, length = raw.shape
    return pl.pallas_call(
        functools.partial(exchange_kernel, tm_count, chan_count, freq_count),
        out_shape=pltpu.VMEM((3, groups, 2 * ROWS, LANES), jnp.bfloat16),
        in_specs=[pl.BlockSpec(memory_space=pltpu.HBM)] * 3,
        out_specs=pl.BlockSpec(memory_space=pltpu.VMEM),
        scratch_shapes=[
            pltpu.VMEM(table.shape, jnp.bfloat16),
            pltpu.VMEM((width, length), jnp.bfloat16),
            pltpu.VMEM((1, width), jnp.int32),
            pltpu.VMEM((groups, 2 * ROWS, LANES), jnp.bfloat16),
            pltpu.SemaphoreType.DMA((2, TIME_CHUNKS)),
            pltpu.SemaphoreType.DMA,
            pltpu.SemaphoreType.DMA,
            pltpu.SemaphoreType.DMA((PARTS,)),
            pltpu.SemaphoreType.DMA((2, PARTS)),
            pltpu.SemaphoreType.DMA((2, PARTS)),
            pltpu.SemaphoreType.DMA((PARTS,)),
            pltpu.SemaphoreType.REGULAR,
        ],
        compiler_params=pltpu.CompilerParams(
            collective_id=0, has_side_effects=True, vmem_limit_bytes=16 << 20
        ),
        name="exchange",
    )(*(pltpu.with_memory_space_constraint(x, pltpu.HBM) for x in (table, raw, mask)))


def channel_of(row):
    return row // 8 * 8 + 7 - row % 8


def band_kernel(blocks_ref, reach_ref, out_ref, right_v, left_v, reach_v, band_v, out_sem):
    depth = right_v.shape[0]
    row = lax.broadcasted_iota(jnp.int32, (LANES, LANES), 0)
    lane = lax.broadcasted_iota(jnp.int32, (LANES, LANES), 1)
    order = (channel_of(row) == lane).astype(jnp.bfloat16)
    for block in range(3):
        tiles = blocks_ref[block].astype(jnp.float32)
        for half in range(2):
            at = (2 * block + half) * LANES
            piece = tiles[:, half * ROWS:(half + 1) * ROWS, :]
            right_v[:, at:at + LANES] = piece.reshape(depth, LANES).astype(jnp.bfloat16)
            if block == 0:
                turned = jnp.concatenate([-piece[:, FB_DEV:], piece[:, :FB_DEV]], axis=1)
                for part, value in enumerate((piece, turned)):
                    left_v[part, at:at + LANES, :] = lax.dot_general(
                        order, value.reshape(depth, LANES).astype(jnp.bfloat16), (((1,), (1,)), ((), ())),
                        preferred_element_type=jnp.float32,
                    ).astype(jnp.bfloat16)
    reach_v[...] = jnp.broadcast_to(reach_ref[...], (LANES, 2 * LANES)).T

    column = lax.broadcasted_iota(jnp.int32, (LANES, depth), 1)
    backwards = 7 - lax.broadcasted_iota(jnp.int32, (8, LANES), 0)
    tiles = K // LANES
    copies = []
    for part in range(2):
        for which in range(FB_DEV):
            for half in range(2):
                rows = slice(half * LANES, (half + 1) * LANES)
                left = jnp.where(column % FB_DEV == which, left_v[part, rows, :], jnp.zeros((), jnp.bfloat16))
                product = jnp.concatenate([
                    jnp.dot(left, right_v[:, at:at + 2 * LANES], preferred_element_type=jnp.float32)
                    for at in range(0, 6 * LANES, 2 * LANES)
                ], axis=1)[:, half * LANES:half * LANES + K + LANES]
                for j in range(tiles):
                    here = product[:, j * LANES:(j + 1) * LANES]
                    beyond = product[:, (j + 1) * LANES:(j + 2) * LANES]
                    joined = jnp.where(lane >= channel_of(row), here, beyond)
                    band = jnp.concatenate([
                        jnp.take_along_axis(
                            pltpu.roll(joined[at:at + 8], (LANES - 7 - at) % LANES, 1, stride=1, stride_axis=0),
                            backwards, axis=0, mode="promise_in_bounds",
                        )
                        for at in range(0, LANES, 8)
                    ], axis=0)
                    band = jnp.where(lane + j * LANES <= reach_v[rows, :], band, 0.0)
                    band_v[part, which, rows, j * LANES:(j + 1) * LANES] = band.astype(jnp.bfloat16)
            copy = pltpu.make_async_copy(band_v.at[part, which], out_ref.at[part, which], out_sem.at[part, which])
            copy.start()
            copies.append(copy)
    for copy in copies:
        copy.wait()


def band_of(blocks, reach):
    depth = blocks.shape[1] * ROWS
    shape = (2, FB_DEV, 2 * LANES, K)
    return pl.pallas_call(
        band_kernel,
        out_shape=jax.ShapeDtypeStruct(shape, jnp.bfloat16),
        in_specs=[pl.BlockSpec(memory_space=pltpu.VMEM)] * 2,
        out_specs=pl.BlockSpec(memory_space=pl.ANY),
        scratch_shapes=[
            pltpu.VMEM((depth, 6 * LANES), jnp.bfloat16),
            pltpu.VMEM((2, 2 * LANES, depth), jnp.bfloat16),
            pltpu.VMEM((2 * LANES, LANES), jnp.int32),
            pltpu.VMEM(shape, jnp.bfloat16),
            pltpu.SemaphoreType.DMA((2, FB_DEV)),
        ],
        compiler_params=pltpu.CompilerParams(vmem_limit_bytes=32 << 20),
        name="band",
    )(blocks, reach)


def body(table, raw_record, good_mask, reach_limit):
    tm_count, chan_count, freq_count = (lax.axis_size(a) for a in ("tm", "chan", "freq"))
    width = raw_record.shape[1]
    blocks = exchange(table, raw_record[0], good_mask.reshape(1, width), tm_count, chan_count, freq_count)
    return band_of(blocks, reach_limit.reshape(1, width))


def solution(mesh):
    groups = mesh.shape["tm"] * mesh.shape["freq"]
    sharded = jax.shard_map(
        body,
        mesh=mesh,
        in_specs=(P(), P(("tm", "freq"), "chan", None), P("chan"), P("chan")),
        out_specs=P(None, ("tm", "freq"), "chan", None),
        check_vma=False,
    )

    def run(raw_record, good_mask, reach_limit):
        table = jnp.asarray(build_rows(groups, raw_record.shape[2]))
        return sharded(table, raw_record, good_mask, reach_limit)

    return run
```

```python
import functools

import jax
import jax.numpy as jnp
import numpy as np
from jax import lax
from jax.experimental import pallas as pl
from jax.experimental.pallas import tpu as pltpu
from jax.sharding import PartitionSpec as P

K = 512
F0 = 64
FB_DEV = 4
ROWS = 2 * FB_DEV
LANES = 128
TIME_CHUNKS = 4
PARTS = 4
MESH = pl.DeviceIdType.MESH


def build_rows(groups, length):
    bins = F0 + np.arange(groups * FB_DEV, dtype=np.int64)
    times = np.arange(length, dtype=np.int64)
    turn = np.float32(2.0 * np.pi)
    phase = turn * ((bins[:, None] * times[None, :]) % length).astype(np.float32) / np.float32(length)
    taper = np.float32(0.5) - np.float32(0.5) * np.cos(turn * times.astype(np.float32) / np.float32(length))
    real_part = (taper[None, :] * np.cos(phase)).reshape(groups, FB_DEV, length)
    imag_part = (-taper[None, :] * np.sin(phase)).reshape(groups, FB_DEV, length)
    rows = np.stack([real_part, imag_part], axis=1).reshape(groups * ROWS, length)
    return rows.reshape(groups * ROWS, length // LANES, LANES).transpose(1, 0, 2).astype(jnp.bfloat16)


def rank_of(distance, count):
    return jnp.maximum(jnp.minimum(2 * distance - 1, 2 * (count - distance)), 0)


def channel_of(row):
    return row // 8 * 8 + 7 - row % 8


def exchange_kernel(tm_count, chan_count, freq_count, table_ref, raw_ref, mask_ref, right_ref, left_ref,
                    table_v, raw_v, mask_v, send_v, blocks_ref, load_sem, mask_sem, send_sem, recv_sem, ahead_send, ahead_recv, relay_send, go_sem):
    tm, chan, freq = lax.axis_index("tm"), lax.axis_index("chan"), lax.axis_index("freq")
    groups = tm_count * freq_count
    per_part = groups // PARTS

    beside = [(tm, lax.rem(freq + df, freq_count), 0, df) for df in range(1, freq_count)]
    peers = []
    for k in range(tm_count - 1):
        t = k + jnp.minimum(jnp.maximum(k + 1 - tm, 0), 1)
        rank = rank_of(lax.rem(tm - t + tm_count, tm_count), tm_count)
        peers += [(t, lax.rem(freq + df, freq_count), rank, df) for df in range(freq_count)]

    low, high = 5 * tm_count // 16, 10 * tm_count // 16
    split = (low + high) // 2
    far = (tm >= low) & (tm < high)

    length = raw_ref.shape[1]
    step = length // TIME_CHUNKS
    loads = []
    for i in range(TIME_CHUNKS):
        span = pl.ds(i * step, step)
        runs = pl.ds(i * step // LANES, step // LANES)
        loads.append((
            pltpu.make_async_copy(table_ref.at[runs], table_v.at[runs], load_sem.at[0, i]),
            pltpu.make_async_copy(raw_ref.at[:, span], raw_v.at[:, span], load_sem.at[1, i]),
        ))
    for pair in loads:
        for copy in pair:
            copy.start()
    mask_copy = pltpu.make_async_copy(mask_ref, mask_v, mask_sem)
    mask_copy.start()

    barrier = pltpu.get_barrier_semaphore()

    def greet(t, f):
        pl.semaphore_signal(barrier, inc=1, device_id=(t, chan, f), device_id_type=MESH)

    @pl.when(tm < low)
    def _():
        for t, f, _, _ in beside + peers:
            greet(t, f)

    @pl.when(far)
    def _():
        for t in (*range(low), *range(high, tm_count)):
            for f in range(freq_count):
                greet(t, f)

    @pl.when(tm >= high)
    def _():
        for t in (*range(low), *range(high, tm_count - 1)):
            past = jnp.minimum(jnp.maximum(t + 1 - tm, 0), 1)
            for f in range(freq_count):
                greet(t + past, f)
        for t, f, _, _ in beside:
            greet(t, f)

    for up in (1, 2):
        @pl.when(chan + up < chan_count)
        def _():
            pl.semaphore_signal(barrier, inc=1, device_id=(tm, chan + up, freq), device_id_type=MESH)

    for up in (1, 2):
        @pl.when(chan + up >= chan_count)
        def _():
            blocks_ref[up] = jnp.zeros(blocks_ref.shape[1:], blocks_ref.dtype)

    spectrum = None
    for i, pair in enumerate(loads):
        for copy in pair:
            copy.wait()
        rows = jnp.concatenate([table_v[j] for j in range(i * step // LANES, (i + 1) * step // LANES)], axis=1)
        term = lax.dot_general(
            rows, raw_v[:, i * step:(i + 1) * step], (((1,), (1,)), ((), ())), preferred_element_type=jnp.float32
        )
        spectrum = term if spectrum is None else spectrum + term
    power = jnp.sum(spectrum * spectrum, axis=0, keepdims=True) / (groups * FB_DEV)
    mask_copy.wait()
    factor = lax.rsqrt(power + 1e-06) * mask_v[...].astype(jnp.float32)
    white = (spectrum * factor).reshape(groups, ROWS, 2 * LANES)
    tiles = jnp.concatenate([white[:, :, :LANES], white[:, :, LANES:]], axis=1)
    send_v[...] = tiles.astype(jnp.bfloat16)

    def send(some):
        for t, f, rank, df in some:
            pltpu.make_async_remote_copy(
                src_ref=send_v.at[t * freq_count + f],
                dst_ref=blocks_ref.at[0, rank * freq_count + df],
                send_sem=send_sem,
                recv_sem=recv_sem.at[rank * freq_count // per_part],
                device_id=(t, chan, f),
                device_id_type=MESH,
            ).start()

    def let_go(planes):
        for t in planes:
            pl.semaphore_signal(go_sem, inc=1, device_id=(t, chan, freq), device_id_type=MESH)

    @pl.when(far)
    def _():
        pl.semaphore_wait(barrier, low * freq_count + jnp.minimum(chan, 2))

    @pl.when(jnp.logical_not(far))
    def _():
        pl.semaphore_wait(barrier, groups - 1 + jnp.minimum(chan, 2))

    @pl.when(tm == low - 1)
    def _():
        let_go(range(low, split))

    @pl.when(tm == high)
    def _():
        let_go(range(split, high))

    send(peers[:low * freq_count])

    @pl.when(far)
    def _():
        pl.semaphore_wait(go_sem, 1)

    send(beside + peers[low * freq_count:])
    blocks_ref[0, 0] = send_v[tm * freq_count + freq]

    odd = lax.rem(chan, 2) == 1

    def ahead(up, q):
        span = pl.ds(q * per_part, per_part)
        return pltpu.make_async_remote_copy(
            src_ref=blocks_ref.at[0, span],
            dst_ref=blocks_ref.at[up, span],
            send_sem=ahead_send.at[up - 1, q],
            recv_sem=ahead_recv.at[up - 1, q],
            device_id=(tm, chan - up, freq),
            device_id_type=MESH,
        )

    for q in range(PARTS):
        lo = 1 if q == 0 else q * per_part
        span = pl.ds(lo, (q + 1) * per_part - lo)
        pltpu.make_async_copy(blocks_ref.at[0, span], blocks_ref.at[0, span], recv_sem.at[q]).wait()
        @pl.when(chan >= 1)
        def _():
            ahead(1, q).start()

        @pl.when((odd if q < 2 else True) & (chan >= 2))
        def _():
            ahead(2, q).start()

    passing = odd & (chan + 1 < chan_count)

    def relay(q):
        span = pl.ds(q * per_part, per_part)
        return pltpu.make_async_remote_copy(
            src_ref=blocks_ref.at[1, span],
            dst_ref=blocks_ref.at[2, span],
            send_sem=relay_send.at[q],
            recv_sem=ahead_recv.at[1, q],
            device_id=(tm, chan - 1, freq),
            device_id_type=MESH,
        )

    depth = groups * ROWS

    def lay_out(block):
        tiles = blocks_ref[block].astype(jnp.float32)
        for half in range(2):
            at = (2 * block + half) * LANES
            piece = tiles[:, half * ROWS:(half + 1) * ROWS, :]
            right_ref[:, at:at + LANES] = piece.reshape(depth, LANES).astype(jnp.bfloat16)
            if block == 0:
                row = lax.broadcasted_iota(jnp.int32, (LANES, LANES), 0)
                lane = lax.broadcasted_iota(jnp.int32, (LANES, LANES), 1)
                order = (channel_of(row) == lane).astype(jnp.bfloat16)
                turned = jnp.concatenate([-piece[:, FB_DEV:], piece[:, :FB_DEV]], axis=1)
                for part, value in enumerate((piece, turned)):
                    left_ref[part, at:at + LANES, :] = lax.dot_general(
                        order, value.reshape(depth, LANES).astype(jnp.bfloat16), (((1,), (1,)), ((), ())),
                        preferred_element_type=jnp.float32,
                    ).astype(jnp.bfloat16)

    lay_out(0)

    @pl.when(passing)
    def _():
        for q in range(PARTS):
            ahead(1, q).wait_recv()
            if q < 2:
                relay(q).start()

    @pl.when(jnp.logical_not(odd))
    def _():
        for q in range(PARTS):
            ahead(1, q).wait_recv()

    lay_out(1)

    @pl.when(chan + 2 < chan_count)
    def _():
        for q in range(PARTS):
            ahead(2, q).wait_recv()

    lay_out(2)

    rest = pl.ds(1, groups - 1)
    pltpu.make_async_copy(send_v.at[rest], send_v.at[rest], send_sem).wait()

    @pl.when(chan >= 1)
    def _():
        for q in range(PARTS):
            ahead(1, q).wait_send()

    @pl.when(odd & (chan >= 2))
    def _():
        for q in range(2):
            ahead(2, q).wait_send()

    @pl.when(chan >= 2)
    def _():
        for q in range(2, PARTS):
            ahead(2, q).wait_send()

    @pl.when(passing)
    def _():
        for q in range(2):
            relay(q).wait_send()


def exchange(table, raw, mask, tm_count, chan_count, freq_count):
    groups = tm_count * freq_count
    width, length = raw.shape
    return pl.pallas_call(
        functools.partial(exchange_kernel, tm_count, chan_count, freq_count),
        out_shape=(
            pltpu.VMEM((groups * ROWS, 6 * LANES), jnp.bfloat16),
            pltpu.VMEM((2, 2 * LANES, groups * ROWS), jnp.bfloat16),
        ),
        in_specs=[pl.BlockSpec(memory_space=pltpu.HBM)] * 3,
        out_specs=(pl.BlockSpec(memory_space=pltpu.VMEM),) * 2,
        scratch_shapes=[
            pltpu.VMEM(table.shape, jnp.bfloat16),
            pltpu.VMEM((width, length), jnp.bfloat16),
            pltpu.VMEM((1, width), jnp.int32),
            pltpu.VMEM((groups, 2 * ROWS, LANES), jnp.bfloat16),
            pltpu.VMEM((3, groups, 2 * ROWS, LANES), jnp.bfloat16),
            pltpu.SemaphoreType.DMA((2, TIME_CHUNKS)),
            pltpu.SemaphoreType.DMA,
            pltpu.SemaphoreType.DMA,
            pltpu.SemaphoreType.DMA((PARTS,)),
            pltpu.SemaphoreType.DMA((2, PARTS)),
            pltpu.SemaphoreType.DMA((2, PARTS)),
            pltpu.SemaphoreType.DMA((PARTS,)),
            pltpu.SemaphoreType.REGULAR,
        ],
        compiler_params=pltpu.CompilerParams(
            collective_id=0, has_side_effects=True, vmem_limit_bytes=16 << 20
        ),
        name="exchange",
    )(*(pltpu.with_memory_space_constraint(x, pltpu.HBM) for x in (table, raw, mask)))


def band_kernel(right_ref, left_ref, reach_ref, out_ref, reach_v, band_v, out_sem):
    depth = right_ref.shape[0]
    row = lax.broadcasted_iota(jnp.int32, (LANES, LANES), 0)
    lane = lax.broadcasted_iota(jnp.int32, (LANES, LANES), 1)
    reach_v[...] = jnp.broadcast_to(reach_ref[...], (LANES, 2 * LANES)).T

    column = lax.broadcasted_iota(jnp.int32, (2 * LANES, depth), 1)
    backwards = 7 - lax.broadcasted_iota(jnp.int32, (8, LANES), 0)
    tiles = K // LANES
    copies = []
    for part in range(2):
        for which in range(FB_DEV):
            left = jnp.where(column % FB_DEV == which, left_ref[part], jnp.zeros((), jnp.bfloat16))
            whole = jnp.concatenate([
                jnp.dot(left, right_ref[:, at:at + 2 * LANES], preferred_element_type=jnp.float32)
                for at in range(0, 6 * LANES, 2 * LANES)
            ], axis=1)
            for half in range(2):
                rows = slice(half * LANES, (half + 1) * LANES)
                product = whole[rows, half * LANES:half * LANES + K + LANES]
                for j in range(tiles):
                    here = product[:, j * LANES:(j + 1) * LANES]
                    beyond = product[:, (j + 1) * LANES:(j + 2) * LANES]
                    joined = jnp.where(lane >= channel_of(row), here, beyond)
                    band = jnp.concatenate([
                        jnp.take_along_axis(
                            pltpu.roll(joined[at:at + 8], (LANES - 7 - at) % LANES, 1, stride=1, stride_axis=0),
                            backwards, axis=0, mode="promise_in_bounds",
                        )
                        for at in range(0, LANES, 8)
                    ], axis=0)
                    band = jnp.where(lane + j * LANES <= reach_v[rows, :], band, 0.0)
                    band_v[part, which, rows, j * LANES:(j + 1) * LANES] = band.astype(jnp.bfloat16)
            copy = pltpu.make_async_copy(band_v.at[part, which], out_ref.at[part, which], out_sem.at[part, which])
            copy.start()
            copies.append(copy)
    for copy in copies:
        copy.wait()


def band_of(right, left, reach):
    shape = (2, FB_DEV, 2 * LANES, K)
    return pl.pallas_call(
        band_kernel,
        out_shape=jax.ShapeDtypeStruct(shape, jnp.bfloat16),
        in_specs=[pl.BlockSpec(memory_space=pltpu.VMEM)] * 3,
        out_specs=pl.BlockSpec(memory_space=pl.ANY),
        scratch_shapes=[
            pltpu.VMEM((2 * LANES, LANES), jnp.int32),
            pltpu.VMEM(shape, jnp.bfloat16),
            pltpu.SemaphoreType.DMA((2, FB_DEV)),
        ],
        compiler_params=pltpu.CompilerParams(vmem_limit_bytes=32 << 20),
        name="band",
    )(right, left, reach)


def body(table, raw_record, good_mask, reach_limit):
    tm_count, chan_count, freq_count = (lax.axis_size(a) for a in ("tm", "chan", "freq"))
    width = raw_record.shape[1]
    right, left = exchange(table, raw_record[0], good_mask.reshape(1, width), tm_count, chan_count, freq_count)
    return band_of(right, left, reach_limit.reshape(1, width))


def solution(mesh):
    groups = mesh.shape["tm"] * mesh.shape["freq"]
    sharded = jax.shard_map(
        body,
        mesh=mesh,
        in_specs=(P(), P(("tm", "freq"), "chan", None), P("chan"), P("chan")),
        out_specs=P(None, ("tm", "freq"), "chan", None),
        check_vma=False,
    )

    def run(raw_record, good_mask, reach_limit):
        table = jnp.asarray(build_rows(groups, raw_record.shape[2]))
        return sharded(table, raw_record, good_mask, reach_limit)

    return run
```

```python
import functools

import jax
import jax.numpy as jnp
import numpy as np
from jax import lax
from jax.experimental import pallas as pl
from jax.experimental.pallas import tpu as pltpu
from jax.sharding import PartitionSpec as P

K = 512
F0 = 64
FB_DEV = 4
ROWS = 2 * FB_DEV
LANES = 128
TIME_CHUNKS = 2
PARTS = 4
MESH = pl.DeviceIdType.MESH


def build_rows(groups, length):
    bins = F0 + np.arange(groups * FB_DEV, dtype=np.int64)
    times = np.arange(length, dtype=np.int64)
    turn = np.float32(2.0 * np.pi)
    phase = turn * ((bins[:, None] * times[None, :]) % length).astype(np.float32) / np.float32(length)
    taper = np.float32(0.5) - np.float32(0.5) * np.cos(turn * times.astype(np.float32) / np.float32(length))
    real_part = (taper[None, :] * np.cos(phase)).reshape(groups, FB_DEV, length)
    imag_part = (-taper[None, :] * np.sin(phase)).reshape(groups, FB_DEV, length)
    rows = np.stack([real_part, imag_part], axis=1).reshape(groups * ROWS, length)
    return rows.reshape(groups * ROWS, length // LANES, LANES).transpose(1, 0, 2).astype(jnp.bfloat16)


def rank_of(distance, count):
    return jnp.maximum(jnp.minimum(2 * distance - 1, 2 * (count - distance)), 0)


def channel_of(row):
    return row // 8 * 8 + 7 - row % 8


def exchange_kernel(tm_count, chan_count, freq_count, table_ref, raw_ref, mask_ref, right_ref, left_ref,
                    table_v, raw_v, mask_v, send_v, blocks_ref, load_sem, mask_sem, send_sem, recv_sem, ahead_send, ahead_recv, relay_send, go_sem):
    tm, chan, freq = lax.axis_index("tm"), lax.axis_index("chan"), lax.axis_index("freq")
    groups = tm_count * freq_count
    per_part = groups // PARTS

    beside = [(tm, lax.rem(freq + df, freq_count), 0, df) for df in range(1, freq_count)]
    peers = []
    for k in range(tm_count - 1):
        t = k + jnp.minimum(jnp.maximum(k + 1 - tm, 0), 1)
        rank = rank_of(lax.rem(tm - t + tm_count, tm_count), tm_count)
        peers += [(t, lax.rem(freq + df, freq_count), rank, df) for df in range(freq_count)]

    low, high = 5 * tm_count // 16, 10 * tm_count // 16
    split = (low + high) // 2
    far = (tm >= low) & (tm < high)

    length = raw_ref.shape[1]
    step = length // TIME_CHUNKS
    loads = []
    for i in range(TIME_CHUNKS):
        span = pl.ds(i * step, step)
        runs = pl.ds(i * step // LANES, step // LANES)
        loads.append((
            pltpu.make_async_copy(table_ref.at[runs], table_v.at[runs], load_sem.at[0, i]),
            pltpu.make_async_copy(raw_ref.at[:, span], raw_v.at[:, span], load_sem.at[1, i]),
        ))
    barrier = pltpu.get_barrier_semaphore()

    def greet(t, f):
        pl.semaphore_signal(barrier, inc=1, device_id=(t, chan, f), device_id_type=MESH)

    @pl.when(tm < low)
    def _():
        for t, f, _, _ in beside + peers:
            greet(t, f)

    @pl.when(tm >= high)
    def _():
        for t in (*range(low), *range(high, tm_count - 1)):
            past = jnp.minimum(jnp.maximum(t + 1 - tm, 0), 1)
            for f in range(freq_count):
                greet(t + past, f)
        for t, f, _, _ in beside:
            greet(t, f)

    for up in (1, 2):
        @pl.when(chan + up < chan_count)
        def _():
            pl.semaphore_signal(barrier, inc=1, device_id=(tm, chan + up, freq), device_id_type=MESH)

    for pair in loads:
        for copy in pair:
            copy.start()
    mask_copy = pltpu.make_async_copy(mask_ref, mask_v, mask_sem)
    mask_copy.start()

    @pl.when(far)
    def _():
        for t in (*range(low), *range(high, tm_count)):
            for f in range(freq_count):
                greet(t, f)

    for up in (1, 2):
        @pl.when(chan + up >= chan_count)
        def _():
            blocks_ref[up] = jnp.zeros(blocks_ref.shape[1:], blocks_ref.dtype)

    spectrum = None
    for i, pair in enumerate(loads):
        for copy in pair:
            copy.wait()
        rows = jnp.concatenate([table_v[j] for j in range(i * step // LANES, (i + 1) * step // LANES)], axis=1)
        term = lax.dot_general(
            rows, raw_v[:, i * step:(i + 1) * step], (((1,), (1,)), ((), ())), preferred_element_type=jnp.float32
        )
        spectrum = term if spectrum is None else spectrum + term
    power = jnp.sum(spectrum * spectrum, axis=0, keepdims=True) / (groups * FB_DEV)
    mask_copy.wait()
    factor = lax.rsqrt(power + 1e-06) * mask_v[...].astype(jnp.float32)
    white = (spectrum * factor).reshape(groups, ROWS, 2 * LANES)
    tiles = jnp.concatenate([white[:, :, :LANES], white[:, :, LANES:]], axis=1)
    send_v[...] = tiles.astype(jnp.bfloat16)

    def send(some):
        for t, f, rank, df in some:
            pltpu.make_async_remote_copy(
                src_ref=send_v.at[t * freq_count + f],
                dst_ref=blocks_ref.at[0, rank * freq_count + df],
                send_sem=send_sem,
                recv_sem=recv_sem.at[rank * freq_count // per_part],
                device_id=(t, chan, f),
                device_id_type=MESH,
            ).start()

    def let_go(planes):
        for t in planes:
            pl.semaphore_signal(go_sem, inc=1, device_id=(t, chan, freq), device_id_type=MESH)

    @pl.when(far)
    def _():
        pl.semaphore_wait(barrier, low * freq_count + jnp.minimum(chan, 2))

    @pl.when(jnp.logical_not(far))
    def _():
        pl.semaphore_wait(barrier, groups - 1 + jnp.minimum(chan, 2))

    @pl.when(tm == low - 1)
    def _():
        let_go(range(low, split))

    @pl.when(tm == high)
    def _():
        let_go(range(split, high))

    send(peers[:low * freq_count])

    @pl.when(far)
    def _():
        pl.semaphore_wait(go_sem, 1)

    send(beside + peers[low * freq_count:])
    blocks_ref[0, 0] = send_v[tm * freq_count + freq]

    odd = lax.rem(chan, 2) == 1

    def ahead(up, q):
        span = pl.ds(q * per_part, per_part)
        return pltpu.make_async_remote_copy(
            src_ref=blocks_ref.at[0, span],
            dst_ref=blocks_ref.at[up, span],
            send_sem=ahead_send.at[up - 1, q],
            recv_sem=ahead_recv.at[up - 1, q],
            device_id=(tm, chan - up, freq),
            device_id_type=MESH,
        )

    for q in range(PARTS):
        lo = 1 if q == 0 else q * per_part
        span = pl.ds(lo, (q + 1) * per_part - lo)
        pltpu.make_async_copy(blocks_ref.at[0, span], blocks_ref.at[0, span], recv_sem.at[q]).wait()
        @pl.when(chan >= 1)
        def _():
            ahead(1, q).start()

        @pl.when((odd if q < 2 else True) & (chan >= 2))
        def _():
            ahead(2, q).start()

    passing = odd & (chan + 1 < chan_count)

    def relay(q):
        span = pl.ds(q * per_part, per_part)
        return pltpu.make_async_remote_copy(
            src_ref=blocks_ref.at[1, span],
            dst_ref=blocks_ref.at[2, span],
            send_sem=relay_send.at[q],
            recv_sem=ahead_recv.at[1, q],
            device_id=(tm, chan - 1, freq),
            device_id_type=MESH,
        )

    depth = groups * ROWS

    def lay_out(block):
        tiles = blocks_ref[block].astype(jnp.float32)
        for half in range(2):
            at = (2 * block + half) * LANES
            piece = tiles[:, half * ROWS:(half + 1) * ROWS, :]
            right_ref[:, at:at + LANES] = piece.reshape(depth, LANES).astype(jnp.bfloat16)
            if block == 0:
                row = lax.broadcasted_iota(jnp.int32, (LANES, LANES), 0)
                lane = lax.broadcasted_iota(jnp.int32, (LANES, LANES), 1)
                order = (channel_of(row) == lane).astype(jnp.bfloat16)
                turned = jnp.concatenate([-piece[:, FB_DEV:], piece[:, :FB_DEV]], axis=1)
                for part, value in enumerate((piece, turned)):
                    left_ref[part, at:at + LANES, :] = lax.dot_general(
                        order, value.reshape(depth, LANES).astype(jnp.bfloat16), (((1,), (1,)), ((), ())),
                        preferred_element_type=jnp.float32,
                    ).astype(jnp.bfloat16)

    @pl.when(passing)
    def _():
        for q in range(2):
            ahead(1, q).wait_recv()
            relay(q).start()

    lay_out(0)

    @pl.when(passing)
    def _():
        for q in range(2, PARTS):
            ahead(1, q).wait_recv()

    @pl.when(jnp.logical_not(odd))
    def _():
        for q in range(PARTS):
            ahead(1, q).wait_recv()

    lay_out(1)

    @pl.when(chan + 2 < chan_count)
    def _():
        for q in range(PARTS):
            ahead(2, q).wait_recv()

    lay_out(2)

    rest = pl.ds(1, groups - 1)
    pltpu.make_async_copy(send_v.at[rest], send_v.at[rest], send_sem).wait()

    @pl.when(chan >= 1)
    def _():
        for q in range(PARTS):
            ahead(1, q).wait_send()

    @pl.when(odd & (chan >= 2))
    def _():
        for q in range(2):
            ahead(2, q).wait_send()

    @pl.when(chan >= 2)
    def _():
        for q in range(2, PARTS):
            ahead(2, q).wait_send()

    @pl.when(passing)
    def _():
        for q in range(2):
            relay(q).wait_send()


def exchange(table, raw, mask, tm_count, chan_count, freq_count):
    groups = tm_count * freq_count
    width, length = raw.shape
    return pl.pallas_call(
        functools.partial(exchange_kernel, tm_count, chan_count, freq_count),
        out_shape=(
            pltpu.VMEM((groups * ROWS, 6 * LANES), jnp.bfloat16),
            pltpu.VMEM((2, 2 * LANES, groups * ROWS), jnp.bfloat16),
        ),
        in_specs=[pl.BlockSpec(memory_space=pltpu.HBM)] * 3,
        out_specs=(pl.BlockSpec(memory_space=pltpu.VMEM),) * 2,
        scratch_shapes=[
            pltpu.VMEM(table.shape, jnp.bfloat16),
            pltpu.VMEM((width, length), jnp.bfloat16),
            pltpu.VMEM((1, width), jnp.int32),
            pltpu.VMEM((groups, 2 * ROWS, LANES), jnp.bfloat16),
            pltpu.VMEM((3, groups, 2 * ROWS, LANES), jnp.bfloat16),
            pltpu.SemaphoreType.DMA((2, TIME_CHUNKS)),
            pltpu.SemaphoreType.DMA,
            pltpu.SemaphoreType.DMA,
            pltpu.SemaphoreType.DMA((PARTS,)),
            pltpu.SemaphoreType.DMA((2, PARTS)),
            pltpu.SemaphoreType.DMA((2, PARTS)),
            pltpu.SemaphoreType.DMA((PARTS,)),
            pltpu.SemaphoreType.REGULAR,
        ],
        compiler_params=pltpu.CompilerParams(
            collective_id=0, has_side_effects=True, vmem_limit_bytes=16 << 20
        ),
        name="exchange",
    )(*(pltpu.with_memory_space_constraint(x, pltpu.HBM) for x in (table, raw, mask)))


def band_kernel(right_ref, left_ref, reach_ref, out_ref, reach_v, band_v, out_sem):
    depth = right_ref.shape[0]
    row = lax.broadcasted_iota(jnp.int32, (LANES, LANES), 0)
    lane = lax.broadcasted_iota(jnp.int32, (LANES, LANES), 1)
    reach_v[...] = jnp.broadcast_to(reach_ref[...], (LANES, 2 * LANES)).T

    column = lax.broadcasted_iota(jnp.int32, (2 * LANES, depth), 1)
    backwards = 7 - lax.broadcasted_iota(jnp.int32, (8, LANES), 0)
    tiles = K // LANES
    copies = []
    for part in range(2):
        for which in range(FB_DEV):
            left = jnp.where(column % FB_DEV == which, left_ref[part], jnp.zeros((), jnp.bfloat16))
            whole = jnp.concatenate([
                jnp.dot(left, right_ref[:, at:at + 2 * LANES], preferred_element_type=jnp.float32)
                for at in range(0, 6 * LANES, 2 * LANES)
            ], axis=1)
            for half in range(2):
                rows = slice(half * LANES, (half + 1) * LANES)
                product = whole[rows, half * LANES:half * LANES + K + LANES]
                for j in range(tiles):
                    here = product[:, j * LANES:(j + 1) * LANES]
                    beyond = product[:, (j + 1) * LANES:(j + 2) * LANES]
                    joined = jnp.where(lane >= channel_of(row), here, beyond)
                    band = jnp.concatenate([
                        jnp.take_along_axis(
                            pltpu.roll(joined[at:at + 8], (LANES - 7 - at) % LANES, 1, stride=1, stride_axis=0),
                            backwards, axis=0, mode="promise_in_bounds",
                        )
                        for at in range(0, LANES, 8)
                    ], axis=0)
                    band = jnp.where(lane + j * LANES <= reach_v[rows, :], band, 0.0)
                    band_v[part, which, rows, j * LANES:(j + 1) * LANES] = band.astype(jnp.bfloat16)
            copy = pltpu.make_async_copy(band_v.at[part, which], out_ref.at[part, which], out_sem.at[part, which])
            copy.start()
            copies.append(copy)
    for copy in copies:
        copy.wait()


def band_of(right, left, reach):
    shape = (2, FB_DEV, 2 * LANES, K)
    return pl.pallas_call(
        band_kernel,
        out_shape=jax.ShapeDtypeStruct(shape, jnp.bfloat16),
        in_specs=[pl.BlockSpec(memory_space=pltpu.VMEM)] * 3,
        out_specs=pl.BlockSpec(memory_space=pl.ANY),
        scratch_shapes=[
            pltpu.VMEM((2 * LANES, LANES), jnp.int32),
            pltpu.VMEM(shape, jnp.bfloat16),
            pltpu.SemaphoreType.DMA((2, FB_DEV)),
        ],
        compiler_params=pltpu.CompilerParams(vmem_limit_bytes=32 << 20),
        name="band",
    )(right, left, reach)


def body(table, raw_record, good_mask, reach_limit):
    tm_count, chan_count, freq_count = (lax.axis_size(a) for a in ("tm", "chan", "freq"))
    width = raw_record.shape[1]
    right, left = exchange(table, raw_record[0], good_mask.reshape(1, width), tm_count, chan_count, freq_count)
    return band_of(right, left, reach_limit.reshape(1, width))


def solution(mesh):
    groups = mesh.shape["tm"] * mesh.shape["freq"]
    sharded = jax.shard_map(
        body,
        mesh=mesh,
        in_specs=(P(), P(("tm", "freq"), "chan", None), P("chan"), P("chan")),
        out_specs=P(None, ("tm", "freq"), "chan", None),
        check_vma=False,
    )

    def run(raw_record, good_mask, reach_limit):
        table = jnp.asarray(build_rows(groups, raw_record.shape[2]))
        return sharded(table, raw_record, good_mask, reach_limit)

    return run
```
